128 devices in a mesh: smp: 64 (over y, z, x), par: 2 (over core).
Axes of the slice: x: 4, y: 4, z: 4, core: 2. Of those that a mesh axis runs over, the one named last changes fastest.
Arguments:
- derivs: bfloat16 [8192, 16384], P('smp', 'par'), may hold values from -40 to 40
- owner_offset: int32 [33], replicated, may hold values from 0 to 63
Outputs:
- gram_tiles: float32 [2112, 128, 128], P('smp', 'par')
The draws below stay inside these ranges and needn't reach their ends.
All inputs are finite; a program needn't handle non-finite values.
Results may differ from the reference program's by a relative error of at most 0.0016.
Values may be sent and summed in bfloat16 or wider, within the bound.
A program may use at most 64 MiB of HBM per device.

```python
import math
import jax
import jax.numpy as jnp
from jax import lax

SB = 128
P_SIZE = 16384
S = 8192
SLOTS = 33
N_SMP = 64


def draw_derivs(key, part):
    key = jax.random.fold_in(key, 11)
    key_mean, key_rows, key_noise = jax.random.split(key, 3)
    column_base = 3.0 * jax.random.normal(key_mean, (1, P_SIZE), jnp.float32)
    row_scale = jnp.exp(jax.random.uniform(key_rows, (S, 1), jnp.float32, math.log(0.5), math.log(2.0)))
    noise = jax.random.normal(key_noise, (S, P_SIZE), jnp.float32)
    values = jnp.clip(column_base + row_scale * noise, -40.0, 40.0)
    return values.astype(jnp.bfloat16)


def touch_ends(entries, own_key, smallest, largest):
    shape = entries.shape
    place = [jax.random.randint(jax.random.fold_in(own_key, axis), (), 0, shape[axis]) for axis in range(len(shape))]
    entries = entries.at[tuple(place)].set(smallest)
    longest = shape.index(max(shape))
    place[longest] = (place[longest] + 1) % shape[longest]
    return entries.at[tuple(place)].set(largest)


def setup_inputs(seed: int = 0) -> dict:
    key_list = jax.random.split(jax.random.key(seed), 3)
    derivs = draw_derivs(jax.random.fold_in(key_list[2], 71), 0)
    owner_offset = touch_ends(jax.random.randint(key_list[1], (SLOTS,), 0, N_SMP), jax.random.fold_in(key_list[1], 1), 0, N_SMP - 1).astype(jnp.int32)
    return {"derivs": derivs, "owner_offset": owner_offset}


def reference(derivs, owner_offset):
    widened = derivs.astype(jnp.float32)
    column_mean = lax.optimization_barrier(jnp.sum(widened, axis=0)) / jnp.float32(S)
    centered = (widened - column_mean).astype(jnp.bfloat16)
    block_stack = centered.reshape(N_SMP, SB, P_SIZE)
    gram_scale = jnp.float32(1.0 / math.sqrt(P_SIZE))
    lag_index = jnp.arange(SLOTS, dtype=jnp.int32)

    def one_tile(pair_index):
        row_block = block_stack[pair_index[0]]
        col_block = block_stack[pair_index[1]]
        product = lax.dot_general(row_block, col_block, (((1,), (1,)), ((), ())), preferred_element_type=jnp.float32)
        return product * gram_scale

    def one_owner(owner):
        row_ids = (owner - owner_offset) % N_SMP
        col_ids = (row_ids - lag_index) % N_SMP
        return lax.map(one_tile, (row_ids.astype(jnp.int32), col_ids.astype(jnp.int32)))
    owners = jnp.arange(N_SMP, dtype=jnp.int32)
    stacked = lax.map(one_owner, owners)
    return stacked.reshape(N_SMP * SLOTS, SB, SB)
```

```python
import functools

import jax
import jax.numpy as jnp
from jax import lax
from jax.experimental import pallas as pl
from jax.experimental.pallas import tpu as pltpu
from jax.sharding import PartitionSpec as P

MESH = pl.DeviceIdType.MESH
LINE = 4
SB = 128
LAGS = 33
PAIRS = 9
CHUNKS = 8
GROUPS = 3
GROUP = LAGS // GROUPS


def kernel(
    offset_ref,
    x_ref,
    out_ref,
    raw,
    cen,
    gram,
    sums,
    mean,
    *rest,
):
    half = SB // 2
    core_out = rest[0:GROUPS]
    core_in = rest[GROUPS : 2 * GROUPS]
    x_in = rest[2 * GROUPS : 3 * GROUPS]
    z_in = rest[3 * GROUPS : 4 * GROUPS]
    y_in = rest[4 * GROUPS : 5 * GROUPS]
    own_sem, a_send, a_recv, g_send, g_recv, m_send, m_recv, t_send, t_recv = rest[5 * GROUPS :]
    kc = raw.shape[-1]
    quarter = kc * CHUNKS

    s = lax.axis_index("smp")
    core = lax.axis_index("par")
    y, z, x = s // 16, (s // 4) % 4, s % 4

    def along(axis, d):
        ny, nz, nx = y, z, x
        if axis == "y":
            ny = (y + d) % 4
        elif axis == "z":
            nz = (z + d) % 4
        else:
            nx = (x + d) % 4
        return (ny * 16 + nz * 4 + nx, core)

    partner = (s, 1 - core)

    barrier = pltpu.get_barrier_semaphore()
    for axis in "xyz":
        for d in (1, 2, 3):
            pl.semaphore_signal(barrier, inc=1, device_id=along(axis, d), device_id_type=MESH)
    pl.semaphore_signal(barrier, inc=1, device_id=partner, device_id_type=MESH)

    ones = jnp.ones((8, SB), jnp.bfloat16)
    for q in range(LINE):
        for c in range(CHUNKS):
            cols = pl.ds(q * quarter + c * kc, kc)
            sums[0, q, c] = jnp.dot(ones, x_ref[:, cols], preferred_element_type=jnp.float32)

    pl.semaphore_wait(barrier, 10)

    def remote(src, dst, send, recv, dev):
        return pltpu.make_async_remote_copy(
            src_ref=src, dst_ref=dst, send_sem=send, recv_sem=recv, device_id=dev, device_id_type=MESH
        )

    def sum_copy(stage, d, src):
        axis = "xzy"[stage]
        return remote(
            src, sums.at[stage + 1, d], m_send.at[stage, d], m_recv.at[stage, d], along(axis, d)
        )

    for d in (1, 2, 3):
        sum_copy(0, d, sums.at[0, (x + d) % 4]).start()

    my_rows = pl.ds(pl.multiple_of(x * SB, SB), SB)

    def cols_of(q, c):
        return pl.ds(pl.multiple_of(q * quarter + c * kc, kc), kc)

    def a2a(c, d):
        return remote(
            x_ref.at[:, cols_of((x + d) % 4, c)],
            raw.at[0, c, my_rows],
            a_send.at[c, d],
            a_recv.at[c, d],
            along("x", d),
        )

    def own_copy(c):
        return pltpu.make_async_copy(x_ref.at[:, cols_of(x, c)], raw.at[0, c, my_rows], own_sem.at[c])

    def issue(c, carry):
        own_copy(c).start()
        for d in (1, 3, 2):
            a2a(c, d).start()
        return carry

    lax.fori_loop(0, CHUNKS, issue, 0)

    def sum_stage(stage, own):
        for d in (1, 2, 3):
            sum_copy(stage, d, own).wait_recv()
        total = own[...]
        for d in (1, 2, 3):
            total = total + sums[stage + 1, d]
        return total

    def gather_copy(c, slot, src_slot, dev):
        return remote(
            raw.at[src_slot, c], raw.at[slot, c], g_send.at[slot, c], g_recv.at[slot, c], dev
        )

    z_next, z_prev = along("z", 1), along("z", 3)
    y_next, y_prev = along("y", 1), along("y", 3)

    def to_z_next(c):
        return gather_copy(c, 3, 0, z_next)

    def to_z_prev(c):
        return gather_copy(c, 1, 0, z_prev)

    def to_y_next(c):
        return gather_copy(c, 4, 0, y_next)

    def to_y_prev(c):
        return gather_copy(c, 6, 0, y_prev)

    def relay_z_next(c):
        return gather_copy(c, 2, 3, z_next)

    def relay_z_prev(c):
        return gather_copy(c, 2, 1, z_prev)

    def relay_y_next(c):
        return gather_copy(c, 5, 4, y_next)

    def relay_y_prev(c):
        return gather_copy(c, 5, 6, y_prev)

    def stage_one(t):
        for d in (1, 2, 3):
            a2a(t, d).wait_recv()
        own_copy(t).wait()
        to_z_next(t).start()
        to_z_prev(t).start()
        to_y_next(t).start()

        @pl.when(t % 2 == 1)
        def _():
            to_y_prev(t).start()

    def stage_two(t):
        to_z_next(t).wait_recv()
        to_z_prev(t).wait_recv()
        to_y_next(t).wait_recv()

        @pl.when(t % 2 == 0)
        def _():
            relay_z_next(t).start()
            relay_y_next(t).start()

        @pl.when(t % 2 == 1)
        def _():
            to_y_prev(t).wait_recv()
            relay_z_prev(t).start()
            relay_y_prev(t).start()

    def stage_three(t):
        relay_z_next(t).wait_recv()
        relay_y_next(t).wait_recv()
        row = mean[t][0:1, :]

        def center(slot, carry):
            for r in range(4):
                rows = pl.ds(r * SB, SB)
                cen[slot, rows] = (raw[slot, t, rows].astype(jnp.float32) - row).astype(jnp.bfloat16)
            return carry

        lax.fori_loop(0, 6, center, 0)

        def pair(lag, carry):
            lag_y, lag_z = lag // 4, lag % 4
            behind = lag_y + (z + lag_z) // 4
            col = jnp.where(behind == 0, 0, behind + 3)
            for i in range(4):
                tile = lax.dot_general(
                    cen[lag_z, pl.ds(i * SB, SB)],
                    cen[col],
                    (((1,), (1,)), ((), ())),
                    preferred_element_type=jnp.float32,
                )
                for j in range(4):
                    part = tile[:, j * SB : (j + 1) * SB]
                    at = lag * 16 + i * 4 + j

                    @pl.when(t == 0)
                    def _():
                        gram[at] = part

                    @pl.when(t > 0)
                    def _():
                        gram[at] += part

            return carry

        lax.fori_loop(0, PAIRS, pair, 0)

    stage_one(0)
    stage_one(1)
    line_sum = sum_stage(0, sums.at[0, x])
    sums[1, 0] = line_sum
    for d in (1, 2, 3):
        sum_copy(1, d, sums.at[1, 0]).start()
    stage_two(0)
    plane_sum = sum_stage(1, sums.at[1, 0])
    sums[2, 0] = plane_sum
    for d in (1, 2, 3):
        sum_copy(2, d, sums.at[2, 0]).start()
    stage_one(2)
    stage_two(1)
    mean[...] = sum_stage(2, sums.at[2, 0]) * jnp.float32(1.0 / (64 * SB))

    def step(t, carry):
        @pl.when(t + 3 < CHUNKS)
        def _():
            stage_one(t + 3)

        @pl.when(t + 2 < CHUNKS)
        def _():
            stage_two(t + 2)

        stage_three(t)
        return carry

    lax.fori_loop(0, CHUNKS, step, 0)

    def place(k, to_x):
        off = offset_ref[k]
        i = (to_x - off) & 3
        j = (i - k) & 3
        lag = (k - i + j) >> 2
        return off, i, j, lag

    def tail_copy(stage, g, d, src, dst, dev):
        return remote(src, dst, t_send.at[stage, g, d], t_recv.at[stage, g, d], dev)

    def core_copy(g):
        return tail_copy(0, g, 0, core_out[g], core_in[g], partner)

    def x_copy(g, d):
        return tail_copy(1, g, d, core_in[g].at[(x + d) % 4], x_in[g].at[d], along("x", d))

    def z_copy(g, d):
        return tail_copy(2, g, d, z_in[g].at[0], z_in[g].at[d], along("z", d))

    def y_copy(g, d):
        return tail_copy(3, g, d, y_in[g].at[0], y_in[g].at[d], along("y", d))

    their_rows = pl.ds(pl.multiple_of((1 - core) * half, half), half)
    our_rows = pl.ds(pl.multiple_of(core * half, half), half)

    for g in range(GROUPS):

        def pick(e, carry):
            to_x, n = e // GROUP, e % GROUP
            _, i, j, lag = place(g * GROUP + n, to_x)
            core_out[g][to_x, n] = gram[lag * 16 + i * 4 + j, their_rows, :]
            return carry

        lax.fori_loop(0, LINE * GROUP, pick, 0)
        core_copy(g).start()

    for g in range(GROUPS):
        core_copy(g).wait_recv()

        def add(e, carry):
            to_x, n = e // GROUP, e % GROUP
            _, i, j, lag = place(g * GROUP + n, to_x)
            core_in[g][to_x, n] += gram[lag * 16 + i * 4 + j, our_rows, :]
            return carry

        lax.fori_loop(0, LINE * GROUP, add, 0)
        for d in (1, 3, 2):
            x_copy(g, d).start()

    for g in range(GROUPS):
        for d in (1, 2, 3):
            x_copy(g, d).wait_recv()

        def total(n, carry):
            z_in[g][0, n] = (core_in[g][x, n] + x_in[g][1, n]) + (x_in[g][2, n] + x_in[g][3, n])
            return carry

        lax.fori_loop(0, GROUP, total, 0)
        for d in (1, 3, 2):
            z_copy(g, d).start()

    for g in range(GROUPS):
        for d in (1, 2, 3):
            z_copy(g, d).wait_recv()

        def pick_z(n, carry):
            off, i, j, lag = place(g * GROUP + n, x)
            carry_x = (i + (off & 3)) >> 2
            d = ((off >> 2) + carry_x + lag) & 3
            y_in[g][0, n] = z_in[g][d, n]
            return carry

        lax.fori_loop(0, GROUP, pick_z, 0)
        for d in (1, 3, 2):
            y_copy(g, d).start()

    for g in range(GROUPS):
        for d in (1, 2, 3):
            y_copy(g, d).wait_recv()

        def pick_y(n, carry):
            off, i, j, lag = place(g * GROUP + n, x)
            carry_x = (i + (off & 3)) >> 2
            off_z = (off >> 2) & 3
            row_z = (z - off_z - carry_x) & 3
            carry_z = (row_z + off_z + carry_x) >> 2
            d = ((off >> 4) + carry_z) & 3
            out_ref[g * GROUP + n] = y_in[g][d, n] * jnp.float32(1.0 / 128)
            return carry

        lax.fori_loop(0, GROUP, pick_y, 0)

    def drain(c, carry):
        for d in (1, 2, 3):
            a2a(c, d).wait_send()
        to_z_next(c).wait_send()
        to_z_prev(c).wait_send()
        to_y_next(c).wait_send()
        relay_z_next(c).wait_send()
        relay_y_next(c).wait_send()

        @pl.when(c % 2 == 1)
        def _():
            to_y_prev(c).wait_send()

        return carry

    lax.fori_loop(0, CHUNKS, drain, 0)
    for d in (1, 2, 3):
        sum_copy(0, d, sums.at[0, (x + d) % 4]).wait_send()
        sum_copy(1, d, sums.at[1, 0]).wait_send()
        sum_copy(2, d, sums.at[2, 0]).wait_send()
    for g in range(GROUPS):
        core_copy(g).wait_send()
        for d in (1, 2, 3):
            x_copy(g, d).wait_send()
            z_copy(g, d).wait_send()
            y_copy(g, d).wait_send()


def local(derivs, owner_offset):
    rows, params = derivs.shape
    kc = params // LINE // CHUNKS
    half = SB // 2
    tail = lambda n: [pltpu.VMEM((n, GROUP, half, SB), jnp.float32)] * GROUPS
    return pl.pallas_call(
        kernel,
        out_shape=jax.ShapeDtypeStruct((LAGS, half, SB), jnp.float32),
        in_specs=[pl.BlockSpec(memory_space=pltpu.SMEM), pl.BlockSpec(memory_space=pltpu.VMEM)],
        out_specs=pl.BlockSpec(memory_space=pltpu.VMEM),
        scratch_shapes=[
            pltpu.VMEM((7, CHUNKS, 4 * SB, kc), jnp.bfloat16),
            pltpu.VMEM((6, 4 * SB, kc), jnp.bfloat16),
            pltpu.VMEM((PAIRS * 16, SB, SB), jnp.float32),
            pltpu.VMEM((4, LINE, CHUNKS, 8, kc), jnp.float32),
            pltpu.VMEM((CHUNKS, 8, kc), jnp.float32),
            *tail(LINE),
            *tail(LINE),
            *tail(LINE),
            *tail(LINE),
            *tail(LINE),
            pltpu.SemaphoreType.DMA((CHUNKS,)),
            pltpu.SemaphoreType.DMA((CHUNKS, LINE)),
            pltpu.SemaphoreType.DMA((CHUNKS, LINE)),
            pltpu.SemaphoreType.DMA((7, CHUNKS)),
            pltpu.SemaphoreType.DMA((7, CHUNKS)),
            pltpu.SemaphoreType.DMA((3, LINE)),
            pltpu.SemaphoreType.DMA((3, LINE)),
            pltpu.SemaphoreType.DMA((4, GROUPS, LINE)),
            pltpu.SemaphoreType.DMA((4, GROUPS, LINE)),
        ],
        compiler_params=pltpu.CompilerParams(
            collective_id=0, has_side_effects=True, vmem_limit_bytes=62 * 2**20
        ),
        cost_estimate=pl.CostEstimate(flops=10**10, bytes_accessed=4 * 2**20, transcendentals=0),
    )(owner_offset, derivs)


def solution(mesh):
    return jax.shard_map(
        local,
        mesh=mesh,
        in_specs=(P("smp", "par"), P()),
        out_specs=P("smp", "par", None),
        check_vma=False,
    )
```

```python
import functools

import jax
import jax.numpy as jnp
from jax import lax
from jax.experimental import pallas as pl
from jax.experimental.pallas import tpu as pltpu
from jax.sharding import PartitionSpec as P

MESH = pl.DeviceIdType.MESH
LINE = 4
SB = 128
LAGS = 33
PAIRS = 9
CHUNKS = 8
SPANS = ((0, 5), (12, 5), (5, 7), (17, 5), (22, 5), (27, 6))
EARLY = 2
GROUPS = len(SPANS)
UNROLL = 1


def kernel(
    offset_ref,
    x_ref,
    out_ref,
    raw,
    cen,
    gram,
    sums,
    mean,
    *rest,
):
    half = SB // 2
    at_ref, step_ref = rest[:2]
    own_sem, a_send, a_recv, g_send, g_recv, m_send, m_recv, t_send, t_recv = rest[-9:]
    per_group = [rest[2 + n * GROUPS : 2 + (n + 1) * GROUPS] for n in range(11)]
    core_out, core_in, own_part, x_out, x_in, second, third = per_group[:7]
    xs_out, xs_in, second_scale, third_scale = per_group[7:]
    kc = raw.shape[-1]
    quarter = kc * CHUNKS

    s = lax.axis_index("smp")
    core = lax.axis_index("par")
    y, z, x = s // 16, (s // 4) % 4, s % 4

    def along(axis, d):
        ny, nz, nx = y, z, x
        if axis == "y":
            ny = (y + d) % 4
        elif axis == "z":
            nz = (z + d) % 4
        else:
            nx = (x + d) % 4
        return (ny * 16 + nz * 4 + nx, core)

    partner = (s, 1 - core)

    barrier = pltpu.get_barrier_semaphore()
    for axis in "xyz":
        for d in (1, 2, 3):
            pl.semaphore_signal(barrier, inc=1, device_id=along(axis, d), device_id_type=MESH)
    pl.semaphore_signal(barrier, inc=1, device_id=partner, device_id_type=MESH)

    def clear(n, carry):
        gram[n] = jnp.zeros((SB, SB), jnp.float32)
        return carry

    lax.fori_loop(0, PAIRS * 16, clear, 0)

    def tables(k, carry):
        off = offset_ref[k]
        for to_x in range(LINE):
            i = (to_x - off) & 3
            j = (i - k) & 3
            lag = (k - i + j) >> 2
            at_ref[to_x, k] = lag * 16 + i * 4 + j
        i = (x - off) & 3
        lag = (k - i + ((i - k) & 3)) >> 2
        carry_x = (i + (off & 3)) >> 2
        off_z = (off >> 2) & 3
        step_ref[0, k] = (off_z + carry_x + lag) & 3
        row_z = (z - off_z - carry_x) & 3
        step_ref[1, k] = ((off >> 4) + ((row_z + off_z + carry_x) >> 2)) & 3
        row_z = (z + lag) & 3
        step_ref[2, k] = ((off >> 4) + ((row_z + off_z + carry_x) >> 2)) & 3
        return carry

    lax.fori_loop(0, LAGS, tables, 0)

    ones = jnp.ones((8, SB), jnp.bfloat16)
    for q in range(LINE):
        for c in range(CHUNKS):
            cols = pl.ds(q * quarter + c * kc, kc)
            sums[0, q, c] = jnp.dot(ones, x_ref[:, cols], preferred_element_type=jnp.float32)

    pl.semaphore_wait(barrier, 10)

    def remote(src, dst, send, recv, dev):
        return pltpu.make_async_remote_copy(
            src_ref=src, dst_ref=dst, send_sem=send, recv_sem=recv, device_id=dev, device_id_type=MESH
        )

    def sum_copy(stage, d, src):
        axis = "xzy"[stage]
        return remote(
            src, sums.at[stage + 1, d], m_send.at[stage, d], m_recv.at[stage, d], along(axis, d)
        )

    for d in (1, 2, 3):
        sum_copy(0, d, sums.at[0, (x + d) % 4]).start()

    my_rows = pl.ds(pl.multiple_of(x * SB, SB), SB)

    def cols_of(q, c):
        return pl.ds(pl.multiple_of(q * quarter + c * kc, kc), kc)

    def a2a(c, d):
        return remote(
            x_ref.at[:, cols_of((x + d) % 4, c)],
            raw.at[0, c, my_rows],
            a_send.at[c, d],
            a_recv.at[c, d],
            along("x", d),
        )

    def own_copy(c):
        return pltpu.make_async_copy(x_ref.at[:, cols_of(x, c)], raw.at[0, c, my_rows], own_sem.at[c])

    def issue(c, carry):
        own_copy(c).start()
        for d in (1, 3, 2):
            a2a(c, d).start()
        return carry

    lax.fori_loop(0, CHUNKS, issue, 0)

    def sum_stage(stage, own):
        for d in (1, 2, 3):
            sum_copy(stage, d, own).wait_recv()
        total = own[...]
        for d in (1, 2, 3):
            total = total + sums[stage + 1, d]
        return total

    top, bottom = pl.ds(0, 2 * SB), pl.ds(2 * SB, 2 * SB)

    def gather_copy(c, n, slot, src_slot, dev, rows=None):
        src, dst = raw.at[src_slot, c], raw.at[slot, c]
        if rows is not None:
            src, dst = src.at[rows], dst.at[rows]
        return remote(src, dst, g_send.at[n, c], g_recv.at[n, c], dev)

    z_next, z_prev = along("z", 1), along("z", 3)
    y_next, y_prev = along("y", 1), along("y", 3)

    def own_sends(c):
        return [
            gather_copy(c, 0, 3, 0, z_next),
            gather_copy(c, 1, 1, 0, z_prev),
            gather_copy(c, 2, 4, 0, y_next),
            gather_copy(c, 3, 6, 0, y_prev, bottom),
        ]

    def relays(c):
        return [
            gather_copy(c, 4, 2, 3, z_next, top),
            gather_copy(c, 5, 2, 1, z_prev, bottom),
            gather_copy(c, 6, 5, 4, y_next, top),
            gather_copy(c, 7, 5, 6, y_prev, bottom),
        ]

    def stage_one(t):
        for d in (1, 2, 3):
            a2a(t, d).wait_recv()
        own_copy(t).wait()
        for copy in own_sends(t):
            copy.start()

    def stage_two(t):
        for first, second in zip(own_sends(t), relays(t)):
            first.wait_recv()
            second.start()

    def centered(t, slots):
        row = mean[t][0:1, :]
        for slot in slots:
            for r in range(4):
                rows = pl.ds(r * SB, SB)
                cen[slot, rows] = (raw[slot, t, rows].astype(jnp.float32) - row).astype(jnp.bfloat16)

    def products(lag):
        lag_y, lag_z = lag // 4, lag % 4
        behind = lag_y + (z + lag_z) // 4
        col = jnp.where(behind == 0, 0, behind + 3)
        for w in range(2):
            wide = lax.dot_general(
                cen[lag_z],
                cen[col, pl.ds(w * 2 * SB, 2 * SB)],
                (((1,), (1,)), ((), ())),
                preferred_element_type=jnp.float32,
            )
            for i in range(4):
                for j in range(2):
                    gram[lag * 16 + i * 4 + w * 2 + j] += wide[
                        i * SB : (i + 1) * SB, j * SB : (j + 1) * SB
                    ]

    def early(t, carry):
        stage_two(t)
        centered(t, (0, 1, 3, 4))
        lax.fori_loop(0, 2, lambda n, c: (products(n * 3), c)[1], 0)
        lax.fori_loop(0, 2, lambda n, c: (products(n * 3 + 1), c)[1], 0)
        return carry

    def late(t, carry):
        for copy in relays(t):
            copy.wait_recv()
        centered(t, (0, 1, 2, 3, 4, 5))
        products(2)
        lax.fori_loop(5, PAIRS, lambda n, c: (products(n), c)[1], 0)
        return carry

    line_sum = sum_stage(0, sums.at[0, x])
    sums[1, 0] = line_sum
    for d in (1, 2, 3):
        sum_copy(1, d, sums.at[1, 0]).start()
    stage_one(0)
    stage_one(1)
    plane_sum = sum_stage(1, sums.at[1, 0])
    sums[2, 0] = plane_sum
    for d in (1, 2, 3):
        sum_copy(2, d, sums.at[2, 0]).start()

    def spread(t, carry):
        stage_one(t)
        return carry

    lax.fori_loop(2, CHUNKS, spread, 0)
    mean[...] = sum_stage(2, sums.at[2, 0]) * jnp.float32(1.0 / (64 * SB))

    def code(tile):
        top_entry = jnp.maximum(jnp.max(jnp.abs(tile), axis=0, keepdims=True), 1e-30)
        scaled = tile * (32767.0 / top_entry)
        return jnp.round(scaled).astype(jnp.int32).astype(jnp.int16), top_entry * (1.0 / 32767.0)

    def decode(tile, scale):
        return tile.astype(jnp.int32).astype(jnp.float32) * scale

    def core_copy(g):
        return remote(core_out[g], core_in[g], t_send.at[0, g, 0], t_recv.at[0, g, 0], partner)

    def pair_copy(stage, g, d, tiles_src, tiles_dst, scale_src, scale_dst, axis):
        dev = along(axis, d)
        return [
            remote(tiles_src, tiles_dst, t_send.at[stage, g, d], t_recv.at[stage, g, d], dev),
            remote(scale_src, scale_dst, t_send.at[stage + 3, g, d], t_recv.at[stage + 3, g, d], dev),
        ]

    def x_copy(g, d):
        to = (x + d) % 4
        return pair_copy(1, g, d, x_out[g].at[to], x_in[g].at[d], xs_out[g].at[to], xs_in[g].at[d], "x")

    axes = ["zy", "yz"] * (GROUPS // 2)

    def second_copy(g, d):
        buf, scale = second[g], second_scale[g]
        return pair_copy(2, g, d, buf.at[0], buf.at[d], scale.at[0], scale.at[d], axes[g][0])

    def third_copy(g, d):
        buf, scale = third[g], third_scale[g]
        return pair_copy(3, g, d, buf.at[0], buf.at[d], scale.at[0], scale.at[d], axes[g][1])

    their_rows = pl.ds(pl.multiple_of((1 - core) * half, half), half)
    our_rows = pl.ds(pl.multiple_of(core * half, half), half)

    def over(count, body):
        lax.fori_loop(0, count, lambda n, c: (body(n), c)[1], 0, unroll=UNROLL)

    def to_partner(g):
        first, count = SPANS[g]
        for to_x in range(LINE):

            def pick(n):
                core_out[g][to_x, n] = gram[at_ref[to_x, first + n], their_rows, :]

            over(count, pick)
        core_copy(g).start()

    def to_line(g):
        first, count = SPANS[g]
        core_copy(g).wait_recv()
        for d in (2, 1, 3, 0):
            to_x = (x + d) % 4

            def add(n):
                tile = core_in[g][to_x, n] + gram[at_ref[to_x, first + n], our_rows, :]
                if d == 0:
                    own_part[g][n] = tile
                else:
                    x_out[g][to_x, n], xs_out[g][to_x, n] = code(tile)

            over(count, add)
            if d:
                for copy in x_copy(g, d):
                    copy.start()

    def to_second(g):
        first, count = SPANS[g]
        for d in (1, 2, 3):
            for copy in x_copy(g, d):
                copy.wait_recv()

        def total(n):
            tile = own_part[g][n]
            for d in (1, 2, 3):
                tile = tile + decode(x_in[g][d, n], xs_in[g][d, n])
            second[g][0, n], second_scale[g][0, n] = code(tile)

        over(count, total)
        for d in (2, 1, 3):
            for copy in second_copy(g, d):
                copy.start()

    def to_third(g):
        first, count = SPANS[g]
        for d in (1, 2, 3):
            for copy in second_copy(g, d):
                copy.wait_recv()

        def pick(n):
            d = step_ref[0 if axes[g][0] == "z" else 2, first + n]
            third[g][0, n] = second[g][d, n]
            third_scale[g][0, n] = second_scale[g][d, n]

        over(count, pick)
        for d in (2, 1, 3):
            for copy in third_copy(g, d):
                copy.start()

    def to_out(g):
        first, count = SPANS[g]
        for d in (1, 2, 3):
            for copy in third_copy(g, d):
                copy.wait_recv()

        def pick(n):
            d = step_ref[0 if axes[g][1] == "z" else 1, first + n]
            out_ref[first + n] = decode(third[g][d, n], third_scale[g][d, n] * jnp.float32(1.0 / 128))

        over(count, pick)

    early_groups, late_groups = range(EARLY), range(EARLY, GROUPS)
    lax.fori_loop(0, CHUNKS, early, 0)
    for g in early_groups:
        to_partner(g)
    for g in early_groups:
        to_line(g)
    lax.fori_loop(0, CHUNKS // 2, late, 0)
    for g in early_groups:
        to_second(g)
    lax.fori_loop(CHUNKS // 2, CHUNKS, late, 0)
    for g in late_groups:
        to_partner(g)
    for g in early_groups:
        to_third(g)
    for step in range(GROUPS - EARLY + 3):
        for delay, stage in ((0, to_line), (1, to_second), (2, to_third), (3, to_out)):
            g = EARLY + step - delay
            if g in late_groups:
                stage(g)
    for g in early_groups:
        to_out(g)

    def drain(c, carry):
        for d in (1, 2, 3):
            a2a(c, d).wait_send()
        for copy in own_sends(c) + relays(c):
            copy.wait_send()
        return carry

    lax.fori_loop(0, CHUNKS, drain, 0)
    for d in (1, 2, 3):
        sum_copy(0, d, sums.at[0, (x + d) % 4]).wait_send()
        sum_copy(1, d, sums.at[1, 0]).wait_send()
        sum_copy(2, d, sums.at[2, 0]).wait_send()
    for g in range(GROUPS):
        core_copy(g).wait_send()
        for d in (1, 2, 3):
            for copy in x_copy(g, d) + second_copy(g, d) + third_copy(g, d):
                copy.wait_send()


def local(derivs, owner_offset):
    rows, params = derivs.shape
    kc = params // LINE // CHUNKS
    half = SB // 2

    def tiles(dtype, *lead):
        return [pltpu.VMEM((*lead, count, half, SB), dtype) for _, count in SPANS]

    def scales():
        return [pltpu.VMEM((LINE, count, 1, SB), jnp.float32) for _, count in SPANS]

    return pl.pallas_call(
        kernel,
        out_shape=jax.ShapeDtypeStruct((LAGS, half, SB), jnp.float32),
        in_specs=[pl.BlockSpec(memory_space=pltpu.SMEM), pl.BlockSpec(memory_space=pltpu.VMEM)],
        out_specs=pl.BlockSpec(memory_space=pltpu.VMEM),
        scratch_shapes=[
            pltpu.VMEM((7, CHUNKS, 4 * SB, kc), jnp.bfloat16),
            pltpu.VMEM((6, 4 * SB, kc), jnp.bfloat16),
            pltpu.VMEM((PAIRS * 16, SB, SB), jnp.float32),
            pltpu.VMEM((4, LINE, CHUNKS, 8, kc), jnp.float32),
            pltpu.VMEM((CHUNKS, 8, kc), jnp.float32),
            pltpu.SMEM((LINE, LAGS), jnp.int32),
            pltpu.SMEM((3, LAGS), jnp.int32),
            *tiles(jnp.float32, LINE),
            *tiles(jnp.float32, LINE),
            *tiles(jnp.float32),
            *tiles(jnp.int16, LINE),
            *tiles(jnp.int16, LINE),
            *tiles(jnp.int16, LINE),
            *tiles(jnp.int16, LINE),
            *scales(),
            *scales(),
            *scales(),
            *scales(),
            pltpu.SemaphoreType.DMA((CHUNKS,)),
            pltpu.SemaphoreType.DMA((CHUNKS, LINE)),
            pltpu.SemaphoreType.DMA((CHUNKS, LINE)),
            pltpu.SemaphoreType.DMA((8, CHUNKS)),
            pltpu.SemaphoreType.DMA((8, CHUNKS)),
            pltpu.SemaphoreType.DMA((3, LINE)),
            pltpu.SemaphoreType.DMA((3, LINE)),
            pltpu.SemaphoreType.DMA((7, GROUPS, LINE)),
            pltpu.SemaphoreType.DMA((7, GROUPS, LINE)),
        ],
        compiler_params=pltpu.CompilerParams(
            collective_id=0, has_side_effects=True, vmem_limit_bytes=62 * 2**20
        ),
        cost_estimate=pl.CostEstimate(flops=10**10, bytes_accessed=4 * 2**20, transcendentals=0),
    )(owner_offset, derivs)


def solution(mesh):
    return jax.shard_map(
        local,
        mesh=mesh,
        in_specs=(P("smp", "par"), P()),
        out_specs=P("smp", "par", None),
        check_vma=False,
    )
```

```python
import functools

import jax
import jax.numpy as jnp
from jax import lax
from jax.experimental import pallas as pl
from jax.experimental.pallas import tpu as pltpu
from jax.sharding import PartitionSpec as P

MESH = pl.DeviceIdType.MESH
LINE = 4
SB = 128
LAGS = 33
PAIRS = 9
CHUNKS = 8
SPANS = ((0, 5, 0, 0), (12, 5, 0, 0), (17, 4, 0, 0), (28, 5, 0, 0), (5, 4, 0, 0), (9, 3, 0, 0), (21, 4, 0, 0), (25, 3, 0, 0))
PLAN = (
    ("early", (0, 8)),
    ("P", 0),
    ("P", 1),
    ("middle", (0, 1)),
    ("L", 0),
    ("L", 1),
    ("middle", (1, 5)),
    ("late", (0, 4)),
    ("middle", (5, 8)),
    ("P", 2),
    ("P", 3),
    ("late", (4, 5)),
    ("L", 2),
    ("L", 3),
    ("S", 0),
    ("S", 1),
    ("late", (5, 8)),
    ("P", 4),
    ("P", 5),
    ("P", 6),
    ("P", 7),
    ("L", 4),
    ("L", 5),
    ("L", 6),
    ("L", 7),
    ("S", 2),
    ("S", 3),
    ("T", 0),
    ("T", 1),
    ("S", 4),
    ("T", 2),
    ("T", 3),
    ("S", 5),
    ("T", 4),
    ("O", 0),
    ("O", 1),
    ("S", 6),
    ("T", 5),
    ("O", 2),
    ("O", 3),
    ("S", 7),
    ("T", 6),
    ("O", 4),
    ("O", 5),
    ("T", 7),
    ("O", 6),
    ("O", 7),
)
SPLIT = 208
GROUPS = len(SPANS)
UNROLL = 1
EXPO = 16


def kernel(
    offset_ref,
    x_ref,
    out_ref,
    raw,
    cen,
    gram,
    sums,
    mean,
    *rest,
):
    half = SB // 2
    at_ref, step_ref = rest[:2]
    own_sem, a_send, a_recv, g_send, g_recv, m_send, m_recv, t_send, t_recv, o_send, o_recv = rest[-11:]
    per_group = [rest[2 + n * GROUPS : 2 + (n + 1) * GROUPS] for n in range(7)]
    core_out, core_in, own_part, x_out, x_in, second, third = per_group
    kc = raw.shape[-1]
    quarter = kc * CHUNKS

    s = lax.axis_index("smp")
    core = lax.axis_index("par")
    y, z, x = s // 16, (s // 4) % 4, s % 4

    def along(axis, d):
        ny, nz, nx = y, z, x
        if axis == "y":
            ny = (y + d) % 4
        elif axis == "z":
            nz = (z + d) % 4
        else:
            nx = (x + d) % 4
        return (ny * 16 + nz * 4 + nx, core)

    partner = (s, 1 - core)

    barrier = pltpu.get_barrier_semaphore()
    for axis in "xyz":
        for d in (1, 2, 3):
            pl.semaphore_signal(barrier, inc=1, device_id=along(axis, d), device_id_type=MESH)
    pl.semaphore_signal(barrier, inc=1, device_id=partner, device_id_type=MESH)

    def clear(n, carry):
        gram[n] = jnp.zeros((SB, SB), jnp.float32)
        return carry

    lax.fori_loop(0, PAIRS * 16, clear, 0)

    def tables(k, carry):
        off = offset_ref[k]
        for to_x in range(LINE):
            i = (to_x - off) & 3
            j = (i - k) & 3
            lag = (k - i + j) >> 2
            at_ref[to_x, k] = lag * 16 + ((x - i) & 3) * 4 + ((x - j) & 3)
        i = (x - off) & 3
        lag = (k - i + ((i - k) & 3)) >> 2
        carry_x = (i + (off & 3)) >> 2
        off_z = (off >> 2) & 3
        step_ref[0, k] = (off_z + carry_x + lag) & 3
        row_z = (z - off_z - carry_x) & 3
        step_ref[1, k] = ((off >> 4) + ((row_z + off_z + carry_x) >> 2)) & 3
        row_z = (z + lag) & 3
        step_ref[2, k] = ((off >> 4) + ((row_z + off_z + carry_x) >> 2)) & 3
        return carry

    lax.fori_loop(0, LAGS, tables, 0)

    def cols_of(q, c):
        return pl.ds(pl.multiple_of(q * quarter + c * kc, kc), kc)

    def own_copy(c):
        return pltpu.make_async_copy(
            x_ref.at[:, cols_of(x, c)], raw.at[0, c, pl.ds(0, SB)], own_sem.at[c]
        )

    for c in range(CHUNKS):
        own_copy(c).start()

    ones = jnp.ones((8, SB), jnp.bfloat16)
    for q in range(LINE):
        for c in range(CHUNKS):
            cols = pl.ds(q * quarter + c * kc, kc)
            sums[0, q, c] = jnp.dot(ones, x_ref[:, cols], preferred_element_type=jnp.float32)

    for c in range(CHUNKS):
        own_copy(c).wait()
    pl.semaphore_wait(barrier, 10)

    def remote(src, dst, send, recv, dev):
        return pltpu.make_async_remote_copy(
            src_ref=src, dst_ref=dst, send_sem=send, recv_sem=recv, device_id=dev, device_id_type=MESH
        )

    def sum_copy(stage, d, src):
        axis = "xzy"[stage]
        return remote(
            src, sums.at[stage + 1, d], m_send.at[stage, d], m_recv.at[stage, d], along(axis, d)
        )

    def a2a(c, d):
        return remote(
            x_ref.at[:, cols_of((x + d) % 4, c)],
            raw.at[0, c, pl.ds(d * SB, SB)],
            a_send.at[c, d],
            a_recv.at[c, d],
            along("x", d),
        )

    def sum_stage(stage, own):
        for d in (1, 2, 3):
            sum_copy(stage, d, own).wait_recv()
        total = own[...]
        for d in (1, 2, 3):
            total = total + sums[stage + 1, d]
        return total

    own_rows, others = pl.ds(0, SB), pl.ds(SB, 3 * SB)
    top, bottom = pl.ds(0, 2 * SB), pl.ds(2 * SB, 2 * SB)
    up, down = pl.ds(0, SPLIT), pl.ds(SPLIT, 4 * SB - SPLIT)

    def gather_copy(c, n, slot, src_slot, dev, rows):
        return remote(
            raw.at[src_slot, c, rows], raw.at[slot, c, rows], g_send.at[n, c], g_recv.at[n, c], dev
        )

    z_next, z_prev = along("z", 1), along("z", 3)
    y_next, y_prev = along("y", 1), along("y", 3)

    near = ((3, z_next), (1, z_prev), (4, y_next))

    def first_sends():
        return [
            remote(raw.at[0, :, own_rows], raw.at[slot, :, own_rows], o_send.at[n], o_recv.at[n], dev)
            for n, (slot, dev) in enumerate(near)
        ]

    def own_sends(c):
        return [gather_copy(c, n, slot, 0, dev, others) for n, (slot, dev) in enumerate(near)] + [
            gather_copy(c, 3, 6, 0, y_prev, down)
        ]

    def y_relays(c):
        return [gather_copy(c, 4, 5, 4, y_next, up), gather_copy(c, 5, 5, 6, y_prev, down)]

    def z_relays(c):
        return [gather_copy(c, 6, 2, 3, z_next, top), gather_copy(c, 7, 2, 1, z_prev, bottom)]

    def stage_one(t):
        for d in (1, 2, 3):
            a2a(t, d).wait_recv()
        for copy in own_sends(t):
            copy.start()

    def stage_two(t):
        for copy in own_sends(t):
            copy.wait_recv()
        for copy in y_relays(t) + z_relays(t):
            copy.start()

    def centered(t, slots):
        row = mean[t][0:1, :]
        for slot in slots:
            for r in range(4):
                rows = pl.ds(r * SB, SB)
                cen[slot, rows] = (raw[slot, t, rows].astype(jnp.float32) - row).astype(jnp.bfloat16)

    def products(lag):
        lag_y, lag_z = lag // 4, lag % 4
        behind = lag_y + (z + lag_z) // 4
        col = jnp.where(behind == 0, 0, behind + 3)
        for w in range(2):
            wide = lax.dot_general(
                cen[lag_z],
                cen[col, pl.ds(w * 2 * SB, 2 * SB)],
                (((1,), (1,)), ((), ())),
                preferred_element_type=jnp.float32,
            )
            for i in range(4):
                for j in range(2):
                    gram[lag * 16 + i * 4 + w * 2 + j] += wide[
                        i * SB : (i + 1) * SB, j * SB : (j + 1) * SB
                    ]

    def early(t, carry):
        stage_two(t)
        centered(t, (0, 1, 3, 4))
        lax.fori_loop(0, 2, lambda n, c: (products(n * 3), c)[1], 0)
        lax.fori_loop(0, 2, lambda n, c: (products(n * 3 + 1), c)[1], 0)
        return carry

    def middle(t, carry):
        for copy in y_relays(t):
            copy.wait_recv()
        centered(t, (0, 1, 3, 4, 5))
        products(5)
        lax.fori_loop(7, PAIRS, lambda n, c: (products(n), c)[1], 0)
        return carry

    def late(t, carry):
        for copy in z_relays(t):
            copy.wait_recv()
        centered(t, (0, 2, 4, 5))
        lax.fori_loop(0, 2, lambda n, c: (products(2 + 4 * n), c)[1], 0)
        return carry

    for copy in first_sends():
        copy.start()
    for d in (1, 2, 3):
        sum_copy(0, d, sums.at[0, (x + d) % 4]).start()

    def issue(c, carry):
        for d in (2, 1, 3):
            a2a(c, d).start()
        return carry

    lax.fori_loop(0, CHUNKS, issue, 0)

    line_sum = sum_stage(0, sums.at[0, x])
    sums[1, 0] = line_sum
    for d in (1, 2, 3):
        sum_copy(1, d, sums.at[1, 0]).start()

    def spread(t, carry):
        stage_one(t)
        return carry

    lax.fori_loop(0, CHUNKS // 2, spread, 0)
    plane_sum = sum_stage(1, sums.at[1, 0])
    sums[2, 0] = plane_sum
    for d in (1, 2, 3):
        sum_copy(2, d, sums.at[2, 0]).start()
    lax.fori_loop(CHUNKS // 2, CHUNKS, spread, 0)
    for copy in first_sends():
        copy.wait_recv()
    mean[...] = sum_stage(2, sums.at[2, 0]) * jnp.float32(1.0 / (64 * SB))

    row_id = lax.broadcasted_iota(jnp.int32, (EXPO, SB), 0)
    no_rows = jnp.zeros((EXPO, SB), jnp.int32)

    def count_of(g):
        return SPANS[g][1] + SPANS[g][2]

    def lag_of(g, n):
        first, count, _, more = SPANS[g]
        return first + n + jnp.where(n >= count, more - first - count, 0)

    def tile_rows(n):
        return pl.ds(pl.multiple_of(n * half, half), half)

    def last_rows(g):
        return pl.ds(count_of(g) * half, EXPO)

    def code(tile):
        top_entry = jnp.maximum(jnp.max(jnp.abs(tile), axis=0, keepdims=True), 1e-30)
        expo = jnp.ceil(jnp.log2(top_entry))
        scaled = tile * (jnp.exp2(-expo) * 32000.0)
        return jnp.round(scaled).astype(jnp.int32).astype(jnp.int16), expo.astype(jnp.int32)

    def exponents(buf, g, d, n):
        rows = buf[g][d, last_rows(g), :].astype(jnp.int32)
        return jnp.sum(jnp.where(row_id == n, rows, 0), axis=0, keepdims=True)

    def decode(buf, g, d, n, factor):
        expo = exponents(buf, g, d, n).astype(jnp.float32)
        tile = buf[g][d, tile_rows(n), :].astype(jnp.int32).astype(jnp.float32)
        return tile * (jnp.exp2(expo) * (factor / 32000.0))

    def core_copy(g):
        return remote(core_out[g], core_in[g], t_send.at[0, g, 0], t_recv.at[0, g, 0], partner)

    def coded_copy(stage, g, d, src, dst, axis):
        return remote(src, dst, t_send.at[stage, g, d], t_recv.at[stage, g, d], along(axis, d))

    def x_copy(g, d):
        return coded_copy(1, g, d, x_out[g].at[(x + d) % 4], x_in[g].at[d], "x")

    axes = ('zy', 'yz', 'zy', 'yz', 'zy', 'yz', 'zy', 'yz')

    def second_copy(g, d):
        return coded_copy(2, g, d, second[g].at[0], second[g].at[d], axes[g][0])

    def third_copy(g, d):
        return coded_copy(3, g, d, third[g].at[0], third[g].at[d], axes[g][1])

    their_rows = pl.ds(pl.multiple_of((1 - core) * half, half), half)
    our_rows = pl.ds(pl.multiple_of(core * half, half), half)

    def over(g, body, init=0):
        return lax.fori_loop(0, count_of(g), body, init, unroll=UNROLL)

    def to_partner(g):
        for to_x in range(LINE):

            def pick(n, carry):
                core_out[g][to_x, n] = gram[at_ref[to_x, lag_of(g, n)], their_rows, :]
                return carry

            over(g, pick)
        core_copy(g).start()

    def to_line(g):
        core_copy(g).wait_recv()
        for d in (2, 1, 3, 0):
            to_x = (x + d) % 4

            def add(n, rows):
                tile = core_in[g][to_x, n] + gram[at_ref[to_x, lag_of(g, n)], our_rows, :]
                if d == 0:
                    own_part[g][n] = tile
                    return rows
                x_out[g][to_x, tile_rows(n)], expo = code(tile)
                return jnp.where(row_id == n, expo, rows)

            rows = over(g, add, no_rows)
            if d:
                x_out[g][to_x, last_rows(g)] = rows.astype(jnp.int16)
                x_copy(g, d).start()

    def to_second(g):
        for d in (1, 2, 3):
            x_copy(g, d).wait_recv()

        def total(n, rows):
            tile = own_part[g][n]
            for d in (1, 2, 3):
                tile = tile + decode(x_in, g, d, n, 1.0)
            second[g][0, tile_rows(n)], expo = code(tile)
            return jnp.where(row_id == n, expo, rows)

        second[g][0, last_rows(g)] = over(g, total, no_rows).astype(jnp.int16)
        for d in (2, 1, 3):
            second_copy(g, d).start()

    def to_third(g):
        for d in (1, 2, 3):
            second_copy(g, d).wait_recv()

        def pick(n, rows):
            d = step_ref[0 if axes[g][0] == "z" else 2, lag_of(g, n)]
            third[g][0, tile_rows(n)] = second[g][d, tile_rows(n), :]
            return jnp.where(row_id == n, second[g][d, last_rows(g), :].astype(jnp.int32), rows)

        third[g][0, last_rows(g)] = over(g, pick, no_rows).astype(jnp.int16)
        for d in (2, 1, 3):
            third_copy(g, d).start()

    def to_out(g):
        for d in (1, 2, 3):
            third_copy(g, d).wait_recv()

        def pick(n, carry):
            k = lag_of(g, n)
            d = step_ref[0 if axes[g][1] == "z" else 1, k]
            out_ref[k] = decode(third, g, d, n, 1.0 / 128)
            return carry

        over(g, pick)

    steps = {"P": to_partner, "L": to_line, "S": to_second, "T": to_third, "O": to_out}
    for stage, g in PLAN:
        if stage == "early":
            lax.fori_loop(*g, early, 0)
        elif stage == "middle":
            lax.fori_loop(*g, middle, 0)
        elif stage == "late":
            lax.fori_loop(*g, late, 0)
        else:
            steps[stage](g)

    def drain(c, carry):
        for d in (1, 2, 3):
            a2a(c, d).wait_send()
        for copy in own_sends(c) + y_relays(c) + z_relays(c):
            copy.wait_send()
        return carry

    lax.fori_loop(0, CHUNKS, drain, 0)
    for copy in first_sends():
        copy.wait_send()
    for d in (1, 2, 3):
        sum_copy(0, d, sums.at[0, (x + d) % 4]).wait_send()
        sum_copy(1, d, sums.at[1, 0]).wait_send()
        sum_copy(2, d, sums.at[2, 0]).wait_send()
    for g in range(GROUPS):
        core_copy(g).wait_send()
        for d in (1, 2, 3):
            x_copy(g, d).wait_send()
            second_copy(g, d).wait_send()
            third_copy(g, d).wait_send()


def local(derivs, owner_offset):
    rows, params = derivs.shape
    kc = params // LINE // CHUNKS
    half = SB // 2

    def tiles(*lead):
        return [pltpu.VMEM((*lead, span[1] + span[2], half, SB), jnp.float32) for span in SPANS]

    def coded():
        return [pltpu.VMEM((LINE, (span[1] + span[2]) * half + EXPO, SB), jnp.int16) for span in SPANS]

    return pl.pallas_call(
        kernel,
        out_shape=jax.ShapeDtypeStruct((LAGS, half, SB), jnp.float32),
        in_specs=[pl.BlockSpec(memory_space=pltpu.SMEM), pl.BlockSpec(memory_space=pltpu.VMEM)],
        out_specs=pl.BlockSpec(memory_space=pltpu.VMEM),
        scratch_shapes=[
            pltpu.VMEM((7, CHUNKS, 4 * SB, kc), jnp.bfloat16),
            pltpu.VMEM((6, 4 * SB, kc), jnp.bfloat16),
            pltpu.VMEM((PAIRS * 16, SB, SB), jnp.float32),
            pltpu.VMEM((4, LINE, CHUNKS, 8, kc), jnp.float32),
            pltpu.VMEM((CHUNKS, 8, kc), jnp.float32),
            pltpu.SMEM((LINE, LAGS), jnp.int32),
            pltpu.SMEM((3, LAGS), jnp.int32),
            *tiles(LINE),
            *tiles(LINE),
            *tiles(),
            *coded(),
            *coded(),
            *coded(),
            *coded(),
            pltpu.SemaphoreType.DMA((CHUNKS,)),
            pltpu.SemaphoreType.DMA((CHUNKS, LINE)),
            pltpu.SemaphoreType.DMA((CHUNKS, LINE)),
            pltpu.SemaphoreType.DMA((8, CHUNKS)),
            pltpu.SemaphoreType.DMA((8, CHUNKS)),
            pltpu.SemaphoreType.DMA((3, LINE)),
            pltpu.SemaphoreType.DMA((3, LINE)),
            pltpu.SemaphoreType.DMA((4, GROUPS, LINE)),
            pltpu.SemaphoreType.DMA((4, GROUPS, LINE)),
            pltpu.SemaphoreType.DMA((3,)),
            pltpu.SemaphoreType.DMA((3,)),
        ],
        compiler_params=pltpu.CompilerParams(
            collective_id=0, has_side_effects=True, vmem_limit_bytes=62 * 2**20
        ),
        cost_estimate=pl.CostEstimate(flops=10**10, bytes_accessed=4 * 2**20, transcendentals=0),
    )(owner_offset, derivs)


def solution(mesh):
    return jax.shard_map(
        local,
        mesh=mesh,
        in_specs=(P("smp", "par"), P()),
        out_specs=P("smp", "par", None),
        check_vma=False,
    )
```

```python
import functools

import jax
import jax.numpy as jnp
from jax import lax
from jax.experimental import pallas as pl
from jax.experimental.pallas import tpu as pltpu
from jax.sharding import PartitionSpec as P

MESH = pl.DeviceIdType.MESH
LINE = 4
SB = 128
LAGS = 33
PAIRS = 9
CHUNKS = 8
SPANS = ((0, 5, 0, 0), (12, 5, 0, 0), (17, 4, 0, 0), (28, 5, 0, 0), (5, 4, 0, 0), (9, 3, 0, 0), (21, 4, 0, 0), (25, 3, 0, 0))
PLAN = (
    ("early", (0, 8)),
    ("P", 0),
    ("P", 1),
    ("middle", (0, 1)),
    ("L", 0),
    ("L", 1),
    ("middle", (1, 5)),
    ("late", (0, 4)),
    ("middle", (5, 8)),
    ("P", 2),
    ("P", 3),
    ("late", (4, 5)),
    ("L", 2),
    ("L", 3),
    ("S", 0),
    ("S", 1),
    ("late", (5, 8)),
    ("P", 4),
    ("P", 5),
    ("P", 6),
    ("P", 7),
    ("L", 4),
    ("L", 5),
    ("L", 6),
    ("L", 7),
    ("S", 2),
    ("S", 3),
    ("T", 0),
    ("T", 1),
    ("S", 4),
    ("T", 2),
    ("T", 3),
    ("S", 5),
    ("T", 4),
    ("O", 0),
    ("O", 1),
    ("S", 6),
    ("T", 5),
    ("O", 2),
    ("O", 3),
    ("S", 7),
    ("T", 6),
    ("O", 4),
    ("O", 5),
    ("T", 7),
    ("O", 6),
    ("O", 7),
)
SPLIT = 208
GROUPS = len(SPANS)
UNROLL = 1
EXPO = 16


def kernel(
    offset_ref,
    x_ref,
    out_ref,
    raw,
    cen,
    gram,
    sums,
    mean,
    *rest,
):
    half = SB // 2
    at_ref, step_ref = rest[:2]
    own_sem, a_send, a_recv, g_send, g_recv, m_send, m_recv, t_send, t_recv, o_send, o_recv = rest[-11:]
    per_group = [rest[2 + n * GROUPS : 2 + (n + 1) * GROUPS] for n in range(7)]
    core_out, core_in, own_part, x_out, x_in, second, third = per_group
    kc = raw.shape[-1]
    quarter = kc * CHUNKS

    s = lax.axis_index("smp")
    core = lax.axis_index("par")
    y, z, x = s // 16, (s // 4) % 4, s % 4

    def along(axis, d):
        ny, nz, nx = y, z, x
        if axis == "y":
            ny = (y + d) % 4
        elif axis == "z":
            nz = (z + d) % 4
        else:
            nx = (x + d) % 4
        return (ny * 16 + nz * 4 + nx, core)

    partner = (s, 1 - core)

    barrier = pltpu.get_barrier_semaphore()
    for axis in "xyz":
        for d in (1, 2, 3):
            pl.semaphore_signal(barrier, inc=1, device_id=along(axis, d), device_id_type=MESH)
    pl.semaphore_signal(barrier, inc=1, device_id=partner, device_id_type=MESH)

    def clear(n, carry):
        gram[n] = jnp.zeros((SB, SB), jnp.float32)
        return carry

    lax.fori_loop(0, PAIRS * 16, clear, 0)

    def tables(k, carry):
        off = offset_ref[k]
        for to_x in range(LINE):
            i = (to_x - off) & 3
            j = (i - k) & 3
            lag = (k - i + j) >> 2
            at_ref[to_x, k] = lag * 16 + ((x - i) & 3) * 4 + ((x - j) & 3)
        i = (x - off) & 3
        lag = (k - i + ((i - k) & 3)) >> 2
        carry_x = (i + (off & 3)) >> 2
        off_z = (off >> 2) & 3
        step_ref[0, k] = (off_z + carry_x + lag) & 3
        row_z = (z - off_z - carry_x) & 3
        step_ref[1, k] = ((off >> 4) + ((row_z + off_z + carry_x) >> 2)) & 3
        row_z = (z + lag) & 3
        step_ref[2, k] = ((off >> 4) + ((row_z + off_z + carry_x) >> 2)) & 3
        return carry

    lax.fori_loop(0, LAGS, tables, 0)

    def cols_of(q, c):
        return pl.ds(pl.multiple_of(q * quarter + c * kc, kc), kc)

    def own_copy(c):
        return pltpu.make_async_copy(
            x_ref.at[:, cols_of(x, c)], raw.at[0, c, pl.ds(0, SB)], own_sem.at[c]
        )

    for c in range(CHUNKS):
        own_copy(c).start()

    ones = jnp.ones((8, SB), jnp.bfloat16)
    for q in range(LINE):
        for c in range(CHUNKS):
            cols = pl.ds(q * quarter + c * kc, kc)
            sums[0, q, c] = jnp.dot(ones, x_ref[:, cols], preferred_element_type=jnp.float32)

    for c in range(CHUNKS):
        own_copy(c).wait()
    pl.semaphore_wait(barrier, 10)

    def remote(src, dst, send, recv, dev):
        return pltpu.make_async_remote_copy(
            src_ref=src, dst_ref=dst, send_sem=send, recv_sem=recv, device_id=dev, device_id_type=MESH
        )

    def sum_copy(stage, d, src):
        axis = "xzy"[stage]
        return remote(
            src, sums.at[stage + 1, d], m_send.at[stage, d], m_recv.at[stage, d], along(axis, d)
        )

    def a2a(c, d):
        return remote(
            x_ref.at[:, cols_of((x + d) % 4, c)],
            raw.at[0, c, pl.ds(d * SB, SB)],
            a_send.at[c, d],
            a_recv.at[c, d],
            along("x", d),
        )

    def sum_stage(stage, own):
        for d in (1, 2, 3):
            sum_copy(stage, d, own).wait_recv()
        total = own[...]
        for d in (1, 2, 3):
            total = total + sums[stage + 1, d]
        return total

    own_rows, others = pl.ds(0, SB), pl.ds(SB, 3 * SB)
    top, bottom = pl.ds(0, 2 * SB), pl.ds(2 * SB, 2 * SB)
    up, down = pl.ds(0, SPLIT), pl.ds(SPLIT, 4 * SB - SPLIT)

    def gather_copy(c, n, slot, src_slot, dev, rows):
        return remote(
            raw.at[src_slot, c, rows], raw.at[slot, c, rows], g_send.at[n, c], g_recv.at[n, c], dev
        )

    z_next, z_prev = along("z", 1), along("z", 3)
    y_next, y_prev = along("y", 1), along("y", 3)

    near = ((3, z_next), (1, z_prev), (4, y_next))

    def first_sends():
        return [
            remote(raw.at[0, :, own_rows], raw.at[slot, :, own_rows], o_send.at[n], o_recv.at[n], dev)
            for n, (slot, dev) in enumerate(near)
        ]

    def own_sends(c):
        return [gather_copy(c, n, slot, 0, dev, others) for n, (slot, dev) in enumerate(near)] + [
            gather_copy(c, 3, 6, 0, y_prev, down)
        ]

    def y_relays(c):
        return [gather_copy(c, 4, 5, 4, y_next, up), gather_copy(c, 5, 5, 6, y_prev, down)]

    def z_relays(c):
        return [gather_copy(c, 6, 2, 3, z_next, top), gather_copy(c, 7, 2, 1, z_prev, bottom)]

    def stage_one(t):
        for d in (1, 2, 3):
            a2a(t, d).wait_recv()
        for copy in own_sends(t):
            copy.start()

    def stage_two(t):
        for copy in own_sends(t):
            copy.wait_recv()
        for copy in y_relays(t) + z_relays(t):
            copy.start()

    def centered(t, slots):
        row = mean[t][0:1, :]
        for slot in slots:
            for r in range(4):
                rows = pl.ds(r * SB, SB)
                cen[slot, t, rows] = (raw[slot, t, rows].astype(jnp.float32) - row).astype(jnp.bfloat16)

    def products(t, lag):
        lag_y, lag_z = lag // 4, lag % 4
        behind = lag_y + (z + lag_z) // 4
        col = jnp.where(behind == 0, 0, behind + 3)
        for w in range(2):
            wide = lax.dot_general(
                cen[lag_z, t],
                cen[col, t, pl.ds(w * 2 * SB, 2 * SB)],
                (((1,), (1,)), ((), ())),
                preferred_element_type=jnp.float32,
            )
            for i in range(4):
                for j in range(2):
                    gram[lag * 16 + i * 4 + w * 2 + j] += wide[
                        i * SB : (i + 1) * SB, j * SB : (j + 1) * SB
                    ]

    def early(t, carry):
        stage_two(t)
        centered(t, (0, 1, 3, 4))
        lax.fori_loop(0, 2, lambda n, c: (products(t, n * 3), c)[1], 0)
        lax.fori_loop(0, 2, lambda n, c: (products(t, n * 3 + 1), c)[1], 0)
        return carry

    def middle(t, carry):
        for copy in y_relays(t):
            copy.wait_recv()
        centered(t, (5,))
        products(t, 5)
        lax.fori_loop(7, PAIRS, lambda n, c: (products(t, n), c)[1], 0)
        return carry

    def late(t, carry):
        for copy in z_relays(t):
            copy.wait_recv()
        centered(t, (2,))
        lax.fori_loop(0, 2, lambda n, c: (products(t, 2 + 4 * n), c)[1], 0)
        return carry

    for copy in first_sends():
        copy.start()
    for d in (1, 2, 3):
        sum_copy(0, d, sums.at[0, (x + d) % 4]).start()

    def issue(c, carry):
        for d in (2, 1, 3):
            a2a(c, d).start()
        return carry

    lax.fori_loop(0, CHUNKS, issue, 0)

    line_sum = sum_stage(0, sums.at[0, x])
    sums[1, 0] = line_sum
    for d in (1, 2, 3):
        sum_copy(1, d, sums.at[1, 0]).start()

    def spread(t, carry):
        stage_one(t)
        return carry

    lax.fori_loop(0, CHUNKS // 2, spread, 0)
    plane_sum = sum_stage(1, sums.at[1, 0])
    sums[2, 0] = plane_sum
    for d in (1, 2, 3):
        sum_copy(2, d, sums.at[2, 0]).start()
    lax.fori_loop(CHUNKS // 2, CHUNKS, spread, 0)
    for copy in first_sends():
        copy.wait_recv()
    mean[...] = sum_stage(2, sums.at[2, 0]) * jnp.float32(1.0 / (64 * SB))

    row_id = lax.broadcasted_iota(jnp.int32, (EXPO, SB), 0)
    no_rows = jnp.zeros((EXPO, SB), jnp.int32)

    def count_of(g):
        return SPANS[g][1] + SPANS[g][2]

    def lag_of(g, n):
        first, count, _, more = SPANS[g]
        return first + n + jnp.where(n >= count, more - first - count, 0)

    def tile_rows(n):
        return pl.ds(pl.multiple_of(n * half, half), half)

    def last_rows(g):
        return pl.ds(count_of(g) * half, EXPO)

    def code(tile):
        top_entry = jnp.maximum(jnp.max(jnp.abs(tile), axis=0, keepdims=True), 1e-30)
        expo = jnp.ceil(jnp.log2(top_entry))
        scaled = tile * (jnp.exp2(-expo) * 32000.0)
        return jnp.round(scaled).astype(jnp.int32).astype(jnp.int16), expo.astype(jnp.int32)

    def exponents(buf, g, d, n):
        rows = buf[g][d, last_rows(g), :].astype(jnp.int32)
        return jnp.sum(jnp.where(row_id == n, rows, 0), axis=0, keepdims=True)

    def decode(buf, g, d, n, factor):
        expo = exponents(buf, g, d, n).astype(jnp.float32)
        tile = buf[g][d, tile_rows(n), :].astype(jnp.int32).astype(jnp.float32)
        return tile * (jnp.exp2(expo) * (factor / 32000.0))

    def core_copy(g):
        return remote(core_out[g], core_in[g], t_send.at[0, g, 0], t_recv.at[0, g, 0], partner)

    def coded_copy(stage, g, d, src, dst, axis):
        return remote(src, dst, t_send.at[stage, g, d], t_recv.at[stage, g, d], along(axis, d))

    def x_copy(g, d):
        return coded_copy(1, g, d, x_out[g].at[(x + d) % 4], x_in[g].at[d], "x")

    axes = ('zy', 'yz', 'zy', 'yz', 'zy', 'yz', 'zy', 'yz')

    def second_copy(g, d):
        return coded_copy(2, g, d, second[g].at[0], second[g].at[d], axes[g][0])

    def third_copy(g, d):
        return coded_copy(3, g, d, third[g].at[0], third[g].at[d], axes[g][1])

    their_rows = pl.ds(pl.multiple_of((1 - core) * half, half), half)
    our_rows = pl.ds(pl.multiple_of(core * half, half), half)

    def over(g, body, init=0):
        return lax.fori_loop(0, count_of(g), body, init, unroll=UNROLL)

    def to_partner(g):
        for to_x in range(LINE):

            def pick(n, carry):
                core_out[g][to_x, n] = gram[at_ref[to_x, lag_of(g, n)], their_rows, :]
                return carry

            over(g, pick)
        core_copy(g).start()

    def to_line(g):
        core_copy(g).wait_recv()
        for d in (2, 1, 3, 0):
            to_x = (x + d) % 4

            def add(n, rows):
                tile = core_in[g][to_x, n] + gram[at_ref[to_x, lag_of(g, n)], our_rows, :]
                if d == 0:
                    own_part[g][n] = tile
                    return rows
                x_out[g][to_x, tile_rows(n)], expo = code(tile)
                return jnp.where(row_id == n, expo, rows)

            rows = over(g, add, no_rows)
            if d:
                x_out[g][to_x, last_rows(g)] = rows.astype(jnp.int16)
                x_copy(g, d).start()

    def to_second(g):
        for d in (1, 2, 3):
            x_copy(g, d).wait_recv()

        def total(n, rows):
            tile = own_part[g][n]
            for d in (1, 2, 3):
                tile = tile + decode(x_in, g, d, n, 1.0)
            second[g][0, tile_rows(n)], expo = code(tile)
            return jnp.where(row_id == n, expo, rows)

        second[g][0, last_rows(g)] = over(g, total, no_rows).astype(jnp.int16)
        for d in (2, 1, 3):
            second_copy(g, d).start()

    def to_third(g):
        for d in (1, 2, 3):
            second_copy(g, d).wait_recv()

        def pick(n, rows):
            d = step_ref[0 if axes[g][0] == "z" else 2, lag_of(g, n)]
            third[g][0, tile_rows(n)] = second[g][d, tile_rows(n), :]
            return jnp.where(row_id == n, second[g][d, last_rows(g), :].astype(jnp.int32), rows)

        third[g][0, last_rows(g)] = over(g, pick, no_rows).astype(jnp.int16)
        for d in (2, 1, 3):
            third_copy(g, d).start()

    def to_out(g):
        for d in (1, 2, 3):
            third_copy(g, d).wait_recv()

        def pick(n, carry):
            k = lag_of(g, n)
            d = step_ref[0 if axes[g][1] == "z" else 1, k]
            out_ref[k] = decode(third, g, d, n, 1.0 / 128)
            return carry

        over(g, pick)

    steps = {"P": to_partner, "L": to_line, "S": to_second, "T": to_third, "O": to_out}
    for stage, g in PLAN:
        if stage == "early":
            lax.fori_loop(*g, early, 0)
        elif stage == "middle":
            lax.fori_loop(*g, middle, 0)
        elif stage == "late":
            lax.fori_loop(*g, late, 0)
        else:
            steps[stage](g)

    def drain(c, carry):
        for d in (1, 2, 3):
            a2a(c, d).wait_send()
        for copy in own_sends(c) + y_relays(c) + z_relays(c):
            copy.wait_send()
        return carry

    lax.fori_loop(0, CHUNKS, drain, 0)
    for copy in first_sends():
        copy.wait_send()
    for d in (1, 2, 3):
        sum_copy(0, d, sums.at[0, (x + d) % 4]).wait_send()
        sum_copy(1, d, sums.at[1, 0]).wait_send()
        sum_copy(2, d, sums.at[2, 0]).wait_send()
    for g in range(GROUPS):
        core_copy(g).wait_send()
        for d in (1, 2, 3):
            x_copy(g, d).wait_send()
            second_copy(g, d).wait_send()
            third_copy(g, d).wait_send()


def local(derivs, owner_offset):
    rows, params = derivs.shape
    kc = params // LINE // CHUNKS
    half = SB // 2

    def tiles(*lead):
        return [pltpu.VMEM((*lead, span[1] + span[2], half, SB), jnp.float32) for span in SPANS]

    def coded():
        return [pltpu.VMEM((LINE, (span[1] + span[2]) * half + EXPO, SB), jnp.int16) for span in SPANS]

    return pl.pallas_call(
        kernel,
        out_shape=jax.ShapeDtypeStruct((LAGS, half, SB), jnp.float32),
        in_specs=[pl.BlockSpec(memory_space=pltpu.SMEM), pl.BlockSpec(memory_space=pltpu.VMEM)],
        out_specs=pl.BlockSpec(memory_space=pltpu.VMEM),
        scratch_shapes=[
            pltpu.VMEM((7, CHUNKS, 4 * SB, kc), jnp.bfloat16),
            pltpu.VMEM((6, CHUNKS, 4 * SB, kc), jnp.bfloat16),
            pltpu.VMEM((PAIRS * 16, SB, SB), jnp.float32),
            pltpu.VMEM((4, LINE, CHUNKS, 8, kc), jnp.float32),
            pltpu.VMEM((CHUNKS, 8, kc), jnp.float32),
            pltpu.SMEM((LINE, LAGS), jnp.int32),
            pltpu.SMEM((3, LAGS), jnp.int32),
            *tiles(LINE),
            *tiles(LINE),
            *tiles(),
            *coded(),
            *coded(),
            *coded(),
            *coded(),
            pltpu.SemaphoreType.DMA((CHUNKS,)),
            pltpu.SemaphoreType.DMA((CHUNKS, LINE)),
            pltpu.SemaphoreType.DMA((CHUNKS, LINE)),
            pltpu.SemaphoreType.DMA((8, CHUNKS)),
            pltpu.SemaphoreType.DMA((8, CHUNKS)),
            pltpu.SemaphoreType.DMA((3, LINE)),
            pltpu.SemaphoreType.DMA((3, LINE)),
            pltpu.SemaphoreType.DMA((4, GROUPS, LINE)),
            pltpu.SemaphoreType.DMA((4, GROUPS, LINE)),
            pltpu.SemaphoreType.DMA((3,)),
            pltpu.SemaphoreType.DMA((3,)),
        ],
        compiler_params=pltpu.CompilerParams(
            collective_id=0, has_side_effects=True, vmem_limit_bytes=62 * 2**20
        ),
        cost_estimate=pl.CostEstimate(flops=10**10, bytes_accessed=4 * 2**20, transcendentals=0),
    )(owner_offset, derivs)


def solution(mesh):
    return jax.shard_map(
        local,
        mesh=mesh,
        in_specs=(P("smp", "par"), P()),
        out_specs=P("smp", "par", None),
        check_vma=False,
    )
```

```python
import functools

import jax
import jax.numpy as jnp
from jax import lax
from jax.experimental import pallas as pl
from jax.experimental.pallas import tpu as pltpu
from jax.sharding import PartitionSpec as P

MESH = pl.DeviceIdType.MESH
LINE = 4
SB = 128
LAGS = 33
PAIRS = 9
CHUNKS = 8
SPANS = ((0, 5, 0, 0), (12, 5, 0, 0), (17, 4, 0, 0), (28, 5, 0, 0), (5, 4, 0, 0), (9, 3, 0, 0), (21, 4, 0, 0), (25, 3, 0, 0))
PLAN = (
    ("early", (0, 8)),
    ("P", 0),
    ("P", 1),
    ("middle", (0, 1)),
    ("L", 0),
    ("L", 1),
    ("middle", (1, 5)),
    ("late", (0, 4)),
    ("middle", (5, 8)),
    ("P", 2),
    ("P", 3),
    ("late", (4, 5)),
    ("L", 2),
    ("L", 3),
    ("S", 0),
    ("S", 1),
    ("late", (5, 8)),
    ("P", 4),
    ("P", 5),
    ("P", 6),
    ("P", 7),
    ("L", 4),
    ("L", 5),
    ("L", 6),
    ("L", 7),
    ("S", 2),
    ("S", 3),
    ("T", 0),
    ("T", 1),
    ("S", 4),
    ("T", 2),
    ("T", 3),
    ("S", 5),
    ("T", 4),
    ("O", 0),
    ("O", 1),
    ("S", 6),
    ("T", 5),
    ("O", 2),
    ("O", 3),
    ("S", 7),
    ("T", 6),
    ("O", 4),
    ("O", 5),
    ("T", 7),
    ("O", 6),
    ("W", 0),
    ("O", 7),
)
SPLIT = 208
GROUPS = len(SPANS)
UNROLL = 1
EXPO = 16


def kernel(
    offset_ref,
    x_ref,
    out_ref,
    raw,
    cen,
    gram,
    sums,
    mean,
    *rest,
):
    half = SB // 2
    at_ref, step_ref = rest[:2]
    own_sem, a_send, a_recv, g_send, g_recv, m_send, m_recv, t_send, t_recv, o_send, o_recv = rest[-11:]
    per_group = [rest[2 + n * GROUPS : 2 + (n + 1) * GROUPS] for n in range(7)]
    core_out, core_in, own_part, x_out, x_in, second, third = per_group
    kc = raw.shape[-1]
    quarter = kc * CHUNKS

    s = lax.axis_index("smp")
    core = lax.axis_index("par")
    y, z, x = s // 16, (s // 4) % 4, s % 4

    def along(axis, d):
        ny, nz, nx = y, z, x
        if axis == "y":
            ny = (y + d) % 4
        elif axis == "z":
            nz = (z + d) % 4
        else:
            nx = (x + d) % 4
        return (ny * 16 + nz * 4 + nx, core)

    partner = (s, 1 - core)

    barrier = pltpu.get_barrier_semaphore()
    for axis in "xyz":
        for d in (1, 2, 3):
            pl.semaphore_signal(barrier, inc=1, device_id=along(axis, d), device_id_type=MESH)
    pl.semaphore_signal(barrier, inc=1, device_id=partner, device_id_type=MESH)

    def clear(n, carry):
        gram[n] = jnp.zeros((SB, SB), jnp.float32)
        return carry

    lax.fori_loop(0, PAIRS * 16, clear, 0)

    def tables(k, carry):
        off = offset_ref[k]
        for to_x in range(LINE):
            i = (to_x - off) & 3
            j = (i - k) & 3
            lag = (k - i + j) >> 2
            at_ref[to_x, k] = lag * 16 + ((x - i) & 3) * 4 + ((x - j) & 3)
        i = (x - off) & 3
        lag = (k - i + ((i - k) & 3)) >> 2
        carry_x = (i + (off & 3)) >> 2
        off_z = (off >> 2) & 3
        step_ref[0, k] = (off_z + carry_x + lag) & 3
        row_z = (z - off_z - carry_x) & 3
        step_ref[1, k] = ((off >> 4) + ((row_z + off_z + carry_x) >> 2)) & 3
        row_z = (z + lag) & 3
        step_ref[2, k] = ((off >> 4) + ((row_z + off_z + carry_x) >> 2)) & 3
        return carry

    lax.fori_loop(0, LAGS, tables, 0)

    def cols_of(q, c):
        return pl.ds(pl.multiple_of(q * quarter + c * kc, kc), kc)

    def own_copy(c):
        return pltpu.make_async_copy(
            x_ref.at[:, cols_of(x, c)], raw.at[0, c, pl.ds(0, SB)], own_sem.at[c]
        )

    for c in range(CHUNKS):
        own_copy(c).start()

    ones = jnp.ones((8, SB), jnp.bfloat16)
    for q in range(LINE):
        for c in range(CHUNKS):
            cols = pl.ds(q * quarter + c * kc, kc)
            sums[0, q, c] = jnp.dot(ones, x_ref[:, cols], preferred_element_type=jnp.float32)

    for c in range(CHUNKS):
        own_copy(c).wait()
    pl.semaphore_wait(barrier, 10)

    def remote(src, dst, send, recv, dev):
        return pltpu.make_async_remote_copy(
            src_ref=src, dst_ref=dst, send_sem=send, recv_sem=recv, device_id=dev, device_id_type=MESH
        )

    def sum_copy(stage, d, src):
        axis = "xzy"[stage]
        return remote(
            src, sums.at[stage + 1, d], m_send.at[stage, d], m_recv.at[stage, d], along(axis, d)
        )

    def a2a(c, d):
        return remote(
            x_ref.at[:, cols_of((x + d) % 4, c)],
            raw.at[0, c, pl.ds(d * SB, SB)],
            a_send.at[c, d],
            a_recv.at[c, d],
            along("x", d),
        )

    def sum_stage(stage, own):
        for d in (1, 2, 3):
            sum_copy(stage, d, own).wait_recv()
        total = own[...]
        for d in (1, 2, 3):
            total = total + sums[stage + 1, d]
        return total

    own_rows, others = pl.ds(0, SB), pl.ds(SB, 3 * SB)
    top, bottom = pl.ds(0, 2 * SB), pl.ds(2 * SB, 2 * SB)
    up, down = pl.ds(0, SPLIT), pl.ds(SPLIT, 4 * SB - SPLIT)

    def gather_copy(c, n, slot, src_slot, dev, rows):
        return remote(
            raw.at[src_slot, c, rows], raw.at[slot, c, rows], g_send.at[n, c], g_recv.at[n, c], dev
        )

    z_next, z_prev = along("z", 1), along("z", 3)
    y_next, y_prev = along("y", 1), along("y", 3)

    near = ((3, z_next), (1, z_prev), (4, y_next))

    def first_sends():
        return [
            remote(raw.at[0, :, own_rows], raw.at[slot, :, own_rows], o_send.at[n], o_recv.at[n], dev)
            for n, (slot, dev) in enumerate(near)
        ]

    def own_sends(c):
        return [gather_copy(c, n, slot, 0, dev, others) for n, (slot, dev) in enumerate(near)] + [
            gather_copy(c, 3, 6, 0, y_prev, down)
        ]

    def y_relays(c):
        return [gather_copy(c, 4, 5, 4, y_next, up), gather_copy(c, 5, 5, 6, y_prev, down)]

    def z_relays(c):
        return [gather_copy(c, 6, 2, 3, z_next, top), gather_copy(c, 7, 2, 1, z_prev, bottom)]

    def stage_one(t):
        for d in (1, 2, 3):
            a2a(t, d).wait_recv()
        for copy in own_sends(t):
            copy.start()

    def stage_two(t):
        for copy in own_sends(t):
            copy.wait_recv()
        for copy in y_relays(t) + z_relays(t):
            copy.start()

    def centered(t, slots):
        row = mean[t][0:1, :]
        for slot in slots:
            for r in range(4):
                rows = pl.ds(r * SB, SB)
                cen[slot, t, rows] = (raw[slot, t, rows].astype(jnp.float32) - row).astype(jnp.bfloat16)

    def products(t, lag):
        lag_y, lag_z = lag // 4, lag % 4
        behind = lag_y + (z + lag_z) // 4
        col = jnp.where(behind == 0, 0, behind + 3)
        for w in range(2):
            wide = lax.dot_general(
                cen[lag_z, t],
                cen[col, t, pl.ds(w * 2 * SB, 2 * SB)],
                (((1,), (1,)), ((), ())),
                preferred_element_type=jnp.float32,
            )
            for i in range(4):
                for j in range(2):
                    gram[lag * 16 + i * 4 + w * 2 + j] += wide[
                        i * SB : (i + 1) * SB, j * SB : (j + 1) * SB
                    ]

    def early(t, carry):
        stage_two(t)
        centered(t, (0, 1, 3, 4))
        lax.fori_loop(0, 2, lambda n, c: (products(t, n * 3), c)[1], 0)
        lax.fori_loop(0, 2, lambda n, c: (products(t, n * 3 + 1), c)[1], 0)
        return carry

    def middle(t, carry):
        for copy in y_relays(t):
            copy.wait_recv()
        centered(t, (5,))
        products(t, 5)
        lax.fori_loop(7, PAIRS, lambda n, c: (products(t, n), c)[1], 0)
        return carry

    def late(t, carry):
        for copy in z_relays(t):
            copy.wait_recv()
        centered(t, (2,))
        lax.fori_loop(0, 2, lambda n, c: (products(t, 2 + 4 * n), c)[1], 0)
        return carry

    for copy in first_sends():
        copy.start()
    for d in (1, 2, 3):
        sum_copy(0, d, sums.at[0, (x + d) % 4]).start()

    def issue(c, carry):
        for d in (2, 1, 3):
            a2a(c, d).start()
        return carry

    lax.fori_loop(0, CHUNKS, issue, 0)

    line_sum = sum_stage(0, sums.at[0, x])
    sums[1, 0] = line_sum
    for d in (1, 2, 3):
        sum_copy(1, d, sums.at[1, 0]).start()

    def spread(t, carry):
        stage_one(t)
        return carry

    lax.fori_loop(0, CHUNKS // 2, spread, 0)
    plane_sum = sum_stage(1, sums.at[1, 0])
    sums[2, 0] = plane_sum
    for d in (1, 2, 3):
        sum_copy(2, d, sums.at[2, 0]).start()
    lax.fori_loop(CHUNKS // 2, CHUNKS, spread, 0)
    for copy in first_sends():
        copy.wait_recv()
    mean[...] = sum_stage(2, sums.at[2, 0]) * jnp.float32(1.0 / (64 * SB))

    row_id = lax.broadcasted_iota(jnp.int32, (EXPO, SB), 0)
    no_rows = jnp.zeros((EXPO, SB), jnp.int32)

    def count_of(g):
        return SPANS[g][1] + SPANS[g][2]

    def lag_of(g, n):
        first, count, _, more = SPANS[g]
        return first + n + jnp.where(n >= count, more - first - count, 0)

    def tile_rows(n):
        return pl.ds(pl.multiple_of(n * half, half), half)

    def last_rows(g):
        return pl.ds(count_of(g) * half, EXPO)

    def code(tile):
        top_entry = jnp.maximum(jnp.max(jnp.abs(tile), axis=0, keepdims=True), 1e-30)
        expo = jnp.ceil(jnp.log2(top_entry))
        scaled = tile * (jnp.exp2(-expo) * 32000.0)
        return jnp.round(scaled).astype(jnp.int32).astype(jnp.int16), expo.astype(jnp.int32)

    def exponents(buf, g, d, n):
        rows = buf[g][d, last_rows(g), :].astype(jnp.int32)
        return jnp.sum(jnp.where(row_id == n, rows, 0), axis=0, keepdims=True)

    def decode(buf, g, d, n, factor):
        expo = exponents(buf, g, d, n).astype(jnp.float32)
        tile = buf[g][d, tile_rows(n), :].astype(jnp.int32).astype(jnp.float32)
        return tile * (jnp.exp2(expo) * (factor / 32000.0))

    def core_copy(g):
        return remote(core_out[g], core_in[g], t_send.at[0, g, 0], t_recv.at[0, g, 0], partner)

    def coded_copy(stage, g, d, src, dst, axis):
        return remote(src, dst, t_send.at[stage, g, d], t_recv.at[stage, g, d], along(axis, d))

    def x_copy(g, d):
        return coded_copy(1, g, d, x_out[g].at[(x + d) % 4], x_in[g].at[d], "x")

    axes = ('zy', 'yz', 'zy', 'yz', 'zy', 'yz', 'zy', 'yz')

    def second_copy(g, d):
        return coded_copy(2, g, d, second[g].at[0], second[g].at[d], axes[g][0])

    def third_copy(g, d):
        return coded_copy(3, g, d, third[g].at[0], third[g].at[d], axes[g][1])

    their_rows = pl.ds(pl.multiple_of((1 - core) * half, half), half)
    our_rows = pl.ds(pl.multiple_of(core * half, half), half)

    def over(g, body, init=0):
        return lax.fori_loop(0, count_of(g), body, init, unroll=UNROLL)

    def to_partner(g):
        for to_x in range(LINE):

            def pick(n, carry):
                core_out[g][to_x, n] = gram[at_ref[to_x, lag_of(g, n)], their_rows, :]
                return carry

            over(g, pick)
        core_copy(g).start()

    def to_line(g):
        core_copy(g).wait_recv()
        for d in (2, 1, 3, 0):
            to_x = (x + d) % 4

            def add(n, rows):
                tile = core_in[g][to_x, n] + gram[at_ref[to_x, lag_of(g, n)], our_rows, :]
                if d == 0:
                    own_part[g][n] = tile
                    return rows
                x_out[g][to_x, tile_rows(n)], expo = code(tile)
                return jnp.where(row_id == n, expo, rows)

            rows = over(g, add, no_rows)
            if d:
                x_out[g][to_x, last_rows(g)] = rows.astype(jnp.int16)
                x_copy(g, d).start()

    def to_second(g):
        for d in (1, 2, 3):
            x_copy(g, d).wait_recv()

        def total(n, rows):
            tile = own_part[g][n]
            for d in (1, 2, 3):
                tile = tile + decode(x_in, g, d, n, 1.0)
            second[g][0, tile_rows(n)], expo = code(tile)
            return jnp.where(row_id == n, expo, rows)

        second[g][0, last_rows(g)] = over(g, total, no_rows).astype(jnp.int16)
        for d in (2, 1, 3):
            second_copy(g, d).start()

    def to_third(g):
        for d in (1, 2, 3):
            second_copy(g, d).wait_recv()

        def pick(n, rows):
            d = step_ref[0 if axes[g][0] == "z" else 2, lag_of(g, n)]
            third[g][0, tile_rows(n)] = second[g][d, tile_rows(n), :]
            return jnp.where(row_id == n, second[g][d, last_rows(g), :].astype(jnp.int32), rows)

        third[g][0, last_rows(g)] = over(g, pick, no_rows).astype(jnp.int16)
        for d in (2, 1, 3):
            third_copy(g, d).start()

    def to_out(g):
        for d in (1, 2, 3):
            third_copy(g, d).wait_recv()

        def pick(n, carry):
            k = lag_of(g, n)
            d = step_ref[0 if axes[g][1] == "z" else 1, k]
            out_ref[k] = decode(third, g, d, n, 1.0 / 128)
            return carry

        over(g, pick)

    def settle(_):
        def drain(c, carry):
            for d in (1, 2, 3):
                a2a(c, d).wait_send()
            for copy in own_sends(c) + y_relays(c) + z_relays(c):
                copy.wait_send()
            return carry

        lax.fori_loop(0, CHUNKS, drain, 0)
        for copy in first_sends():
            copy.wait_send()
        for d in (1, 2, 3):
            sum_copy(0, d, sums.at[0, (x + d) % 4]).wait_send()
            sum_copy(1, d, sums.at[1, 0]).wait_send()
            sum_copy(2, d, sums.at[2, 0]).wait_send()
        for g in range(GROUPS):
            core_copy(g).wait_send()
            for d in (1, 2, 3):
                x_copy(g, d).wait_send()
                second_copy(g, d).wait_send()
                if g < GROUPS - 1:
                    third_copy(g, d).wait_send()

    steps = {"P": to_partner, "L": to_line, "S": to_second, "T": to_third, "O": to_out, "W": settle}
    for stage, g in PLAN:
        if stage == "early":
            lax.fori_loop(*g, early, 0)
        elif stage == "middle":
            lax.fori_loop(*g, middle, 0)
        elif stage == "late":
            lax.fori_loop(*g, late, 0)
        else:
            steps[stage](g)

    for d in (1, 2, 3):
        third_copy(GROUPS - 1, d).wait_send()


def local(derivs, owner_offset):
    rows, params = derivs.shape
    kc = params // LINE // CHUNKS
    half = SB // 2

    def tiles(*lead):
        return [pltpu.VMEM((*lead, span[1] + span[2], half, SB), jnp.float32) for span in SPANS]

    def coded():
        return [pltpu.VMEM((LINE, (span[1] + span[2]) * half + EXPO, SB), jnp.int16) for span in SPANS]

    return pl.pallas_call(
        kernel,
        out_shape=jax.ShapeDtypeStruct((LAGS, half, SB), jnp.float32),
        in_specs=[pl.BlockSpec(memory_space=pltpu.SMEM), pl.BlockSpec(memory_space=pltpu.VMEM)],
        out_specs=pl.BlockSpec(memory_space=pltpu.VMEM),
        scratch_shapes=[
            pltpu.VMEM((7, CHUNKS, 4 * SB, kc), jnp.bfloat16),
            pltpu.VMEM((6, CHUNKS, 4 * SB, kc), jnp.bfloat16),
            pltpu.VMEM((PAIRS * 16, SB, SB), jnp.float32),
            pltpu.VMEM((4, LINE, CHUNKS, 8, kc), jnp.float32),
            pltpu.VMEM((CHUNKS, 8, kc), jnp.float32),
            pltpu.SMEM((LINE, LAGS), jnp.int32),
            pltpu.SMEM((3, LAGS), jnp.int32),
            *tiles(LINE),
            *tiles(LINE),
            *tiles(),
            *coded(),
            *coded(),
            *coded(),
            *coded(),
            pltpu.SemaphoreType.DMA((CHUNKS,)),
            pltpu.SemaphoreType.DMA((CHUNKS, LINE)),
            pltpu.SemaphoreType.DMA((CHUNKS, LINE)),
            pltpu.SemaphoreType.DMA((8, CHUNKS)),
            pltpu.SemaphoreType.DMA((8, CHUNKS)),
            pltpu.SemaphoreType.DMA((3, LINE)),
            pltpu.SemaphoreType.DMA((3, LINE)),
            pltpu.SemaphoreType.DMA((4, GROUPS, LINE)),
            pltpu.SemaphoreType.DMA((4, GROUPS, LINE)),
            pltpu.SemaphoreType.DMA((3,)),
            pltpu.SemaphoreType.DMA((3,)),
        ],
        compiler_params=pltpu.CompilerParams(
            collective_id=0, has_side_effects=True, vmem_limit_bytes=62 * 2**20
        ),
        cost_estimate=pl.CostEstimate(flops=10**10, bytes_accessed=4 * 2**20, transcendentals=0),
    )(owner_offset, derivs)


def solution(mesh):
    return jax.shard_map(
        local,
        mesh=mesh,
        in_specs=(P("smp", "par"), P()),
        out_specs=P("smp", "par", None),
        check_vma=False,
    )
```
